32 devices in a mesh: groups: 2 (over x), rows: 16 (over z, y, core).
Axes of the slice: x: 2, y: 2, z: 4, core: 2. Of those that a mesh axis runs over, the one named last changes fastest.
Arguments:
- orbitals: float32 [32768, 1024], P('rows', 'groups'), parts along dimension 1, may hold values from -6 to 6
- trial_orbitals: float32 [32768, 1024], P('rows', 'groups'), parts along dimension 1, may hold values from -0.03125 to 0.03125
- angles: float32 [128], replicated, may hold values from -3.140625 to 3.140625
- horizontal_index: int32 [4, 64, 512], P('groups', 'rows'), parts along dimension 0, may hold values from 0 to 127
- horizontal_mask: int32 [4, 64, 512], P('groups', 'rows'), parts along dimension 0, may hold values 0 or 1
- vertical_index: int32 [8, 64, 512], P('groups', 'rows'), parts along dimension 0, may hold values from 0 to 127
- vertical_mask: int32 [8, 64, 512], P('groups', 'rows'), parts along dimension 0, may hold values 0 or 1
Outputs:
- evolved: float32 [32768, 1024], P('rows', 'groups'), parts along dimension 1
- intersection: float32 [1024, 512], P('groups'), parts along dimension 0
The draws below stay inside these ranges and needn't reach their ends.
There are 2 independent parts, one for each index of `groups`. The reference program is written for one: setup_inputs(seed, part) draws one part's arguments, and reference() takes and returns one part's arrays. A program takes and returns all parts, laid end to end along the dimension named above; an argument that names none is the same for every part. Nothing has to cross between parts.
All inputs are finite; a program needn't handle non-finite values. No bound on the sum of `horizontal_mask` or of `vertical_mask` on one device may be relied on, other than what follows from the above.
Results may differ from the reference program's by a relative error of at most 0.00012.
Values sent between devices are 32-bit elements; how exact they have to be, the bound alone decides.
A program may use at most 128 MiB of HBM per device.

```python
import jax
import jax.numpy as jnp
from jax import lax

LX = 512
COLS = 512
NH = 2
NV = 4
NANG = 128
LY = 64
M = 32768


def set_ends(drawn, rng, least, top_value):
    extent = drawn.shape
    place = [jax.random.randint(jax.random.fold_in(rng, axis), (), 0, extent[axis]) for axis in range(len(extent))]
    drawn = drawn.at[tuple(place)].set(least)
    longest = extent.index(max(extent))
    place[longest] = (place[longest] + 1) % extent[longest]
    return drawn.at[tuple(place)].set(top_value)


def block_levels(rng, shape, shards, least, high):
    level, own = 1.0, jax.random.fold_in(rng, 6)
    for position, blocks in shards:
        heights = jnp.exp(jax.random.uniform(jax.random.fold_in(own, position), (blocks,), jnp.float32, least / len(shards), high / len(shards)))
        level = level * jnp.repeat(heights, shape[position] // blocks).reshape([-1 if axis == position else 1 for axis in range(len(shape))])
    return level


def noise(rng, extent, width, reach, shards=(), held_as=jnp.bfloat16):
    level = block_levels(rng, extent, shards, -0.22, 0.18) if shards else 1.0
    values = jax.random.normal(rng, extent, jnp.float32) * width * level
    return jnp.minimum(jnp.maximum(values, -reach), reach).astype(held_as)


def setup_inputs(seed: int = 0, part: int = 0) -> dict:
    streams_of = jax.random.split(jax.random.key(seed), 8)
    part_keys = jax.random.split(jax.random.fold_in(streams_of[7], part), 8)
    orbitals = noise(part_keys[0], (M, COLS), 1.0, 6.0, ((0, 16),), jnp.float32)
    trial_orbitals = noise(part_keys[1], (M, COLS), (LY * LX) ** -0.5, 0.03125, ((0, 16),), jnp.float32)
    angles = jnp.clip(jax.random.uniform(streams_of[2], (NANG,), jnp.float32, -3.140625, 3.140625), -3.140625, 3.140625)
    horizontal_index = set_ends(jax.random.randint(part_keys[3], (NH, LY, LX), 0, NANG), jax.random.fold_in(part_keys[3], 1), 0, NANG - 1).astype(jnp.int32)
    horizontal_mask = set_ends((jax.random.randint(part_keys[4], (NH, LY, LX), 0, 4) < 3).astype(jnp.int32), jax.random.fold_in(part_keys[4], 1), 0, 1)
    vertical_index = set_ends(jax.random.randint(part_keys[5], (NV, LY, LX), 0, NANG), jax.random.fold_in(part_keys[5], 1), 0, NANG - 1).astype(jnp.int32)
    vertical_mask = set_ends((jax.random.randint(part_keys[6], (NV, LY, LX), 0, 4) < 3).astype(jnp.int32), jax.random.fold_in(part_keys[6], 1), 0, 1)
    return {"orbitals": orbitals, "trial_orbitals": trial_orbitals, "angles": angles, "horizontal_index": horizontal_index, "horizontal_mask": horizontal_mask, "vertical_index": vertical_index, "vertical_mask": vertical_mask}


def coefficients(index, mask, cos_table, sin_table):
    active = mask == 1
    return jnp.where(active, cos_table[index], 1.0), jnp.where(active, sin_table[index], 0.0)


def rotate(first_row, second_row, cosine_part, sine_part):
    cosine_part = cosine_part[..., None]
    sine_part = sine_part[..., None]
    return cosine_part * first_row - sine_part * second_row, sine_part * first_row + cosine_part * second_row


def horizontal_even(current, cosine_part, sine_part):
    first_new, second_new = rotate(current[:, 0::2], current[:, 1::2], cosine_part[:, 0::2], sine_part[:, 0::2])
    return jnp.stack([first_new, second_new], axis=2).reshape(current.shape)


def horizontal(current, cosine_part, sine_part, parity):
    if parity == 0:
        return horizontal_even(current, cosine_part, sine_part)
    interior = horizontal_even(current[:, 1:-1], cosine_part[:, 1:-1], sine_part[:, 1:-1])
    return jnp.concatenate([current[:, :1], interior, current[:, -1:]], axis=1)


def vertical_even(current, cosine_part, sine_part):
    lower_new, partner_new = rotate(current[0::2], jnp.flip(current[1::2], axis=1), cosine_part[0::2], sine_part[0::2])
    upper_new = jnp.flip(partner_new, axis=1)
    return jnp.stack([lower_new, upper_new], axis=1).reshape(current.shape)


def reference(orbitals, trial_orbitals, angles, horizontal_index, horizontal_mask, vertical_index, vertical_mask):
    cos_table = jnp.cos(angles)
    sin_table = jnp.sin(angles)
    across_cos, across_sin = coefficients(horizontal_index, horizontal_mask, cos_table, sin_table)
    upward_cos, upward_sin = coefficients(vertical_index, vertical_mask, cos_table, sin_table)
    current = orbitals.reshape(LY, LX, COLS)
    for layer_index in range(NH):
        current = horizontal(current, across_cos[layer_index], across_sin[layer_index], layer_index % 2)
    for layer_index in range(NV):
        if layer_index % 2 == 0:
            current = vertical_even(current, upward_cos[layer_index], upward_sin[layer_index])
        else:
            rolled = vertical_even(jnp.roll(current, -1, 0), jnp.roll(upward_cos[layer_index], -1, 0), jnp.roll(upward_sin[layer_index], -1, 0))
            current = jnp.roll(rolled, 1, 0)
    evolved = current.reshape(LY * LX, COLS)
    intersection = lax.dot_general(trial_orbitals, evolved, (((0,), (0,)), ((), ())), precision=lax.Precision.HIGHEST, preferred_element_type=jnp.float32)
    return evolved, intersection
```

```python
import functools

import jax
import jax.numpy as jnp
from jax import lax
from jax.experimental import pallas as pl
from jax.experimental.pallas import tpu as pltpu
from jax.sharding import PartitionSpec as P

LANES = 128
BLOCK = 64


def coefficient_kernel(layers_across, layers_up, rows, code_ref, cos_ref, sin_ref, coef_ref, edge_ref):
    count, width = code_ref.shape
    blocks = width // LANES
    cosines, sines = [], []
    for block in range(blocks):
        code = code_ref[:, block * LANES : (block + 1) * LANES]
        place = jnp.maximum(code, 0)
        table_cos = jnp.broadcast_to(cos_ref[...], code.shape)
        table_sin = jnp.broadcast_to(sin_ref[...], code.shape)
        picked_cos = jnp.take_along_axis(table_cos, place, axis=1, mode="promise_in_bounds")
        picked_sin = jnp.take_along_axis(table_sin, place, axis=1, mode="promise_in_bounds")
        cosines.append(jnp.where(code >= 0, picked_cos, 1.0))
        sines.append(jnp.where(code >= 0, picked_sin, 0.0))
    backward = LANES - 1 - lax.broadcasted_iota(jnp.int32, (count, LANES), 1)

    def reverse(parts):
        return [jnp.take_along_axis(part, backward, axis=1, mode="promise_in_bounds") for part in parts[::-1]]

    reverse_cos = jnp.concatenate(reverse(cosines), axis=1)
    reverse_sin = jnp.concatenate(reverse(sines), axis=1)
    cosine = jnp.concatenate(cosines, axis=1)
    sine = jnp.concatenate(sines, axis=1)
    position = lax.broadcasted_iota(jnp.int32, (count, width), 1)
    last_cos = pltpu.roll(cosine, 1, 1)
    last_sin = pltpu.roll(sine, 1, 1)
    diagonals, neighbours = [], []
    for layer in range(layers_across):
        first = position % 2 == layer % 2
        diagonal = jnp.where(first, cosine, last_cos)
        neighbour = jnp.where(first, -sine, last_sin)
        if layer % 2:
            inside = (position > 0) & (position < width - 1)
            diagonal = jnp.where(inside, diagonal, 1.0)
            neighbour = jnp.where(inside, neighbour, 0.0)
        diagonals.append(diagonal)
        neighbours.append(neighbour)
    lanes = coef_ref.shape[2]
    for row in range(rows):
        lines = []
        for layer in range(layers_across):
            at = layer * rows + row
            lines += [diagonals[layer][at : at + 1], neighbours[layer][at : at + 1]]
        for layer in range(layers_up):
            at = (layers_across + layer) * rows + row
            from_cos, from_sin = (reverse_cos, reverse_sin) if row % 2 else (cosine, sine)
            lines += [from_cos[at : at + 1], from_sin[at : at + 1]]
        lines.append(jnp.zeros((lanes - len(lines), width), jnp.float32))
        coef_ref[row] = jnp.transpose(jnp.concatenate(lines, axis=0))
    edges = []
    for layer in range(1, layers_up, 2):
        at = (layers_across + layer) * rows + rows - 1
        edges += [reverse_cos[at : at + 1], reverse_sin[at : at + 1]]
    spare = edge_ref.shape[0] - len(edges)
    if spare:
        edges.append(jnp.zeros((spare, width), jnp.float32))
    edge_ref[...] = jnp.concatenate(edges, axis=0)


def flip(block):
    size, columns = block.shape
    view = block.reshape(size // 8, 8, columns)
    place = lax.broadcasted_iota(jnp.int32, view.shape, 1)
    view = jnp.where(place % 2 == 0, pltpu.roll(view, 7, 1), pltpu.roll(view, 1, 1))
    view = jnp.where(place % 4 < 2, pltpu.roll(view, 6, 1), pltpu.roll(view, 2, 1))
    view = pltpu.roll(view, 4, 1)
    view = jnp.concatenate([view[k : k + 1] for k in range(size // 8)][::-1], axis=0)
    return view.reshape(size, columns)


def split(value):
    high = value.astype(jnp.bfloat16)
    low = (value - high.astype(jnp.float32)).astype(jnp.bfloat16)
    return high, low


def step_kernel(
    devices,
    layers_across,
    layers_up,
    orbital_ref,
    trial_ref,
    coef_ref,
    edge_ref,
    evolved_ref,
    partial_ref,
    state,
    from_last,
    from_next,
    edge_in,
    edge_coef,
    turned,
    trial_high,
    trial_low,
    send_sem,
    recv_sem,
    edge_sem,
):
    rows, width = coef_ref.shape[0], coef_ref.shape[1]
    chunks = state.shape[0]
    steps = width // BLOCK
    stages = layers_up // 2
    me = lax.axis_index("rows")
    after = lax.rem(me + 1, devices)
    before = lax.rem(me + devices - 1, devices)

    barrier = pltpu.get_barrier_semaphore()
    for neighbour in (before, after):
        pl.semaphore_signal(barrier, inc=1, device_id={"rows": neighbour}, device_id_type=pl.DeviceIdType.MESH)
    pl.semaphore_wait(barrier, 2)

    edge_copy = pltpu.make_async_remote_copy(
        src_ref=edge_ref,
        dst_ref=edge_in,
        send_sem=edge_sem.at[0],
        recv_sem=edge_sem.at[1],
        device_id={"rows": after},
        device_id_type=pl.DeviceIdType.MESH,
    )
    edge_copy.start()

    def exchange(stage, chunk):
        down = pltpu.make_async_remote_copy(
            src_ref=state.at[chunk, 0],
            dst_ref=from_next.at[stage, chunk],
            send_sem=send_sem.at[stage, 0, chunk],
            recv_sem=recv_sem.at[stage, 0, chunk],
            device_id={"rows": before},
            device_id_type=pl.DeviceIdType.MESH,
        )
        up = pltpu.make_async_remote_copy(
            src_ref=state.at[chunk, rows - 1],
            dst_ref=from_last.at[stage, chunk],
            send_sem=send_sem.at[stage, 1, chunk],
            recv_sem=recv_sem.at[stage, 1, chunk],
            device_id={"rows": after},
            device_id_type=pl.DeviceIdType.MESH,
        )
        return down, up

    def columns_of(chunk):
        return pl.ds(pl.multiple_of(chunk * LANES, LANES), LANES)

    def vertical(row, layer, place):
        lane = 2 * (layers_across + layer)
        pair = coef_ref[row, place, :]
        return pair[:, lane : lane + 1], pair[:, lane + 1 : lane + 2]

    def open_chunk(chunk, carry):
        columns = columns_of(chunk)
        position = lax.broadcasted_iota(jnp.int32, (width, LANES), 0)
        for row in range(rows):
            value = orbital_ref[pl.ds(row * width, width), columns]
            for layer in range(layers_across):
                diagonal = coef_ref[row, :, 2 * layer : 2 * layer + 1]
                beside = coef_ref[row, :, 2 * layer + 1 : 2 * layer + 2]
                partner = jnp.where(
                    position % 2 == layer % 2, pltpu.roll(value, width - 1, 0), pltpu.roll(value, 1, 0)
                )
                value = diagonal * value + beside * partner
            turned[row] = value

        def pairs(step, carry):
            start = pl.multiple_of(step * BLOCK, BLOCK)
            mirrored = pl.multiple_of(width - BLOCK - step * BLOCK, BLOCK)
            place = pl.ds(start, BLOCK)
            for row in range(0, rows, 2):
                lower = turned[row, place, :]
                upper = flip(turned[row + 1, pl.ds(mirrored, BLOCK), :])
                cosine, sine = vertical(row, 0, place)
                state[chunk, row, place, :] = cosine * lower - sine * upper
                state[chunk, row + 1, place, :] = sine * lower + cosine * upper
            return carry

        lax.fori_loop(0, steps, pairs, 0)
        for copy in exchange(0, chunk):
            copy.start()
        return carry

    lax.fori_loop(0, chunks, open_chunk, 0)

    for row in range(rows):
        place = pl.ds(row * width, width)

        def turn(part, carry):
            columns = columns_of(part)
            high, low = split(jnp.transpose(trial_ref[place, columns]))
            trial_high[columns, place] = high
            trial_low[columns, place] = low
            return carry

        lax.fori_loop(0, trial_ref.shape[1] // LANES, turn, 0)

    edge_copy.wait()
    edge_coef[...] = jnp.transpose(edge_in[...])

    def crossing(stage, chunk, place):
        layer = 2 * stage + 1
        values = [state[chunk, row, place, :] for row in range(rows)]
        edge = edge_coef[place, :]
        edge_cos = edge[:, 2 * stage : 2 * stage + 1]
        edge_sin = edge[:, 2 * stage + 1 : 2 * stage + 2]
        new = list(values)
        new[0] = edge_sin * from_last[stage, chunk, place, :] + edge_cos * values[0]
        for row in range(1, rows - 1, 2):
            cosine, sine = vertical(row, layer, place)
            new[row] = cosine * values[row] - sine * values[row + 1]
            new[row + 1] = sine * values[row] + cosine * values[row + 1]
        cosine, sine = vertical(rows - 1, layer, place)
        new[rows - 1] = cosine * values[rows - 1] - sine * from_next[stage, chunk, place, :]
        return new

    for stage in range(stages):
        final = stage == stages - 1

        def advance(chunk, carry):
            for copy in exchange(stage, chunk):
                copy.wait()

            def middle(step, carry):
                place = pl.ds(pl.multiple_of(step * BLOCK, BLOCK), BLOCK)
                new = crossing(stage, chunk, place)
                for row in range(0, rows, 2):
                    cosine, sine = vertical(row, 2 * stage + 2, place)
                    state[chunk, row, place, :] = cosine * new[row] - sine * new[row + 1]
                    state[chunk, row + 1, place, :] = sine * new[row] + cosine * new[row + 1]
                return carry

            def close(step, carry):
                start = step * BLOCK
                place = pl.ds(pl.multiple_of(start, BLOCK), BLOCK)
                new = crossing(stage, chunk, place)
                for row in range(rows):
                    if row % 2:
                        at = pl.ds(pl.multiple_of((row + 1) * width - BLOCK - start, BLOCK), BLOCK)
                        evolved_ref[at, columns_of(chunk)] = flip(new[row])
                    else:
                        at = pl.ds(pl.multiple_of(row * width + start, BLOCK), BLOCK)
                        evolved_ref[at, columns_of(chunk)] = new[row]
                return carry

            lax.fori_loop(0, steps, close if final else middle, 0)
            if not final:
                for copy in exchange(stage + 1, chunk):
                    copy.start()
                return carry
            total = jnp.zeros((partial_ref.shape[0], LANES), jnp.float32)
            for row in range(rows):
                place = pl.ds(row * width, width)
                high, low = split(evolved_ref[place, columns_of(chunk)])
                total += jnp.dot(trial_high[:, place], high, preferred_element_type=jnp.float32)
                total += jnp.dot(trial_high[:, place], low, preferred_element_type=jnp.float32)
                total += jnp.dot(trial_low[:, place], high, preferred_element_type=jnp.float32)
            partial_ref[:, columns_of(chunk)] = total
            return carry

        lax.fori_loop(0, chunks, advance, 0)


def per_device(
    orbitals,
    trial_orbitals,
    angles,
    horizontal_index,
    horizontal_mask,
    vertical_index,
    vertical_mask,
):
    devices = lax.axis_size("rows")
    layers_across, rows, width = horizontal_index.shape
    layers_up = vertical_index.shape[0]
    modes, columns = orbitals.shape
    trials = trial_orbitals.shape[1]
    chunks = columns // LANES
    stages = layers_up // 2
    code = jnp.concatenate(
        [
            jnp.where(horizontal_mask == 1, horizontal_index, -1).reshape(layers_across * rows, width),
            jnp.where(vertical_mask == 1, vertical_index, -1).reshape(layers_up * rows, width),
        ],
        axis=0,
    )
    lanes = -(-2 * (layers_across + layers_up) // 8) * 8
    edges = -(-2 * stages // 8) * 8
    coef, edge = pl.pallas_call(
        functools.partial(coefficient_kernel, layers_across, layers_up, rows),
        out_shape=(
            jax.ShapeDtypeStruct((rows, width, lanes), jnp.float32),
            jax.ShapeDtypeStruct((edges, width), jnp.float32),
        ),
        name="coefficients",
    )(code, jnp.cos(angles)[None, :], jnp.sin(angles)[None, :])

    in_vmem = pl.BlockSpec(memory_space=pltpu.VMEM)
    evolved, partial_value = pl.pallas_call(
        functools.partial(step_kernel, devices, layers_across, layers_up),
        out_shape=(
            jax.ShapeDtypeStruct((modes, columns), jnp.float32),
            jax.ShapeDtypeStruct((trials, columns), jnp.float32),
        ),
        in_specs=[in_vmem] * 4,
        out_specs=(in_vmem, in_vmem),
        scratch_shapes=[
            pltpu.VMEM((chunks, rows, width, LANES), jnp.float32),
            pltpu.VMEM((stages, chunks, width, LANES), jnp.float32),
            pltpu.VMEM((stages, chunks, width, LANES), jnp.float32),
            pltpu.VMEM((edges, width), jnp.float32),
            pltpu.VMEM((width, edges), jnp.float32),
            pltpu.VMEM((rows, width, LANES), jnp.float32),
            pltpu.VMEM((trials, modes), jnp.bfloat16),
            pltpu.VMEM((trials, modes), jnp.bfloat16),
            pltpu.SemaphoreType.DMA((stages, 2, chunks)),
            pltpu.SemaphoreType.DMA((stages, 2, chunks)),
            pltpu.SemaphoreType.DMA((2,)),
        ],
        compiler_params=pltpu.CompilerParams(
            collective_id=0, has_side_effects=True, vmem_limit_bytes=50 * 1024 * 1024
        ),
        name="trotter_step",
    )(orbitals, trial_orbitals, coef, edge)
    return evolved, lax.psum(partial_value, "rows")


def solution(mesh):
    in_specs = (
        P("rows", "groups"),
        P("rows", "groups"),
        P(),
        P("groups", "rows", None),
        P("groups", "rows", None),
        P("groups", "rows", None),
        P("groups", "rows", None),
    )
    out_specs = (P("rows", "groups"), P("groups", None))
    return jax.shard_map(
        per_device, mesh=mesh, in_specs=in_specs, out_specs=out_specs, check_vma=False
    )
```

```python
import functools

import jax
import jax.numpy as jnp
from jax import lax
from jax.experimental import pallas as pl
from jax.experimental.pallas import tpu as pltpu
from jax.sharding import PartitionSpec as P

LANES = 128
BLOCK = 64


def coefficient_kernel(layers_across, layers_up, rows, code_ref, cos_ref, sin_ref, coef_ref, edge_ref):
    count, width = code_ref.shape
    blocks = width // LANES
    cosines, sines = [], []
    for block in range(blocks):
        code = code_ref[:, block * LANES : (block + 1) * LANES]
        place = jnp.maximum(code, 0)
        table_cos = jnp.broadcast_to(cos_ref[...], code.shape)
        table_sin = jnp.broadcast_to(sin_ref[...], code.shape)
        picked_cos = jnp.take_along_axis(table_cos, place, axis=1, mode="promise_in_bounds")
        picked_sin = jnp.take_along_axis(table_sin, place, axis=1, mode="promise_in_bounds")
        cosines.append(jnp.where(code >= 0, picked_cos, 1.0))
        sines.append(jnp.where(code >= 0, picked_sin, 0.0))
    backward = LANES - 1 - lax.broadcasted_iota(jnp.int32, (count, LANES), 1)

    def reverse(parts):
        return [jnp.take_along_axis(part, backward, axis=1, mode="promise_in_bounds") for part in parts[::-1]]

    reverse_cos = jnp.concatenate(reverse(cosines), axis=1)
    reverse_sin = jnp.concatenate(reverse(sines), axis=1)
    cosine = jnp.concatenate(cosines, axis=1)
    sine = jnp.concatenate(sines, axis=1)
    position = lax.broadcasted_iota(jnp.int32, (count, width), 1)
    last_cos = pltpu.roll(cosine, 1, 1)
    last_sin = pltpu.roll(sine, 1, 1)
    diagonals, neighbours = [], []
    for layer in range(layers_across):
        first = position % 2 == layer % 2
        diagonal = jnp.where(first, cosine, last_cos)
        neighbour = jnp.where(first, -sine, last_sin)
        if layer % 2:
            inside = (position > 0) & (position < width - 1)
            diagonal = jnp.where(inside, diagonal, 1.0)
            neighbour = jnp.where(inside, neighbour, 0.0)
        diagonals.append(diagonal)
        neighbours.append(neighbour)
    lanes = coef_ref.shape[2]
    for row in range(rows):
        lines = []
        for layer in range(layers_across):
            at = layer * rows + row
            lines += [diagonals[layer][at : at + 1], neighbours[layer][at : at + 1]]
        for layer in range(layers_up):
            at = (layers_across + layer) * rows + row
            from_cos, from_sin = (reverse_cos, reverse_sin) if row % 2 else (cosine, sine)
            lines += [from_cos[at : at + 1], from_sin[at : at + 1]]
        lines.append(jnp.zeros((lanes - len(lines), width), jnp.float32))
        coef_ref[row] = jnp.transpose(jnp.concatenate(lines, axis=0))
    edges = []
    for layer in range(1, layers_up, 2):
        at = (layers_across + layer) * rows + rows - 1
        edges += [reverse_cos[at : at + 1], reverse_sin[at : at + 1]]
    spare = edge_ref.shape[0] - len(edges)
    if spare:
        edges.append(jnp.zeros((spare, width), jnp.float32))
    edge_ref[...] = jnp.concatenate(edges, axis=0)


def flip(block):
    size, columns = block.shape
    view = block.reshape(size // 8, 8, columns)
    place = lax.broadcasted_iota(jnp.int32, view.shape, 1)
    view = jnp.where(place % 2 == 0, pltpu.roll(view, 7, 1), pltpu.roll(view, 1, 1))
    view = jnp.where(place % 4 < 2, pltpu.roll(view, 6, 1), pltpu.roll(view, 2, 1))
    view = pltpu.roll(view, 4, 1)
    view = jnp.concatenate([view[k : k + 1] for k in range(size // 8)][::-1], axis=0)
    return view.reshape(size, columns)


def split(value):
    high = value.astype(jnp.bfloat16)
    low = (value - high.astype(jnp.float32)).astype(jnp.bfloat16)
    return high, low


def step_kernel(
    devices,
    layers_across,
    layers_up,
    orbital_ref,
    trial_ref,
    coef_ref,
    edge_ref,
    evolved_ref,
    total_ref,
    state,
    from_last,
    from_next,
    edge_in,
    edge_coef,
    turned,
    trial_high,
    trial_low,
    partial,
    from_twin,
    half,
    from_chips,
    whole,
    send_sem,
    recv_sem,
    edge_sem,
    twin_send,
    twin_recv,
    chip_send,
    chip_recv,
):
    rows, width = coef_ref.shape[0], coef_ref.shape[1]
    chunks = state.shape[0]
    steps = width // BLOCK
    stages = layers_up // 2
    me = lax.axis_index("rows")
    after = lax.rem(me + 1, devices)
    before = lax.rem(me + devices - 1, devices)
    side = lax.rem(me, 2)
    twin = me + 1 - 2 * side
    chips = devices // 2
    chip = me // 2
    depth = partial.shape[1] // devices
    halves = partial.shape[1] // 2

    def chip_at(distance):
        return 2 * lax.rem(chip + distance, chips) + side

    barrier = pltpu.get_barrier_semaphore()
    for neighbour in (before, after):
        pl.semaphore_signal(barrier, inc=1, device_id={"rows": neighbour}, device_id_type=pl.DeviceIdType.MESH)
    for distance in range(1, chips):
        pl.semaphore_signal(
            barrier, inc=1, device_id={"rows": chip_at(distance)}, device_id_type=pl.DeviceIdType.MESH
        )
    pl.semaphore_wait(barrier, 1 + chips)

    edge_copy = pltpu.make_async_remote_copy(
        src_ref=edge_ref,
        dst_ref=edge_in,
        send_sem=edge_sem.at[0],
        recv_sem=edge_sem.at[1],
        device_id={"rows": after},
        device_id_type=pl.DeviceIdType.MESH,
    )
    edge_copy.start()

    def exchange(stage, chunk):
        down = pltpu.make_async_remote_copy(
            src_ref=state.at[chunk, 0],
            dst_ref=from_next.at[stage, chunk],
            send_sem=send_sem.at[stage, 0, chunk],
            recv_sem=recv_sem.at[stage, 0, chunk],
            device_id={"rows": before},
            device_id_type=pl.DeviceIdType.MESH,
        )
        up = pltpu.make_async_remote_copy(
            src_ref=state.at[chunk, rows - 1],
            dst_ref=from_last.at[stage, chunk],
            send_sem=send_sem.at[stage, 1, chunk],
            recv_sem=recv_sem.at[stage, 1, chunk],
            device_id={"rows": after},
            device_id_type=pl.DeviceIdType.MESH,
        )
        return down, up

    def columns_of(chunk):
        return pl.ds(pl.multiple_of(chunk * LANES, LANES), LANES)

    def vertical(row, layer, place):
        lane = 2 * (layers_across + layer)
        pair = coef_ref[row, place, :]
        return pair[:, lane : lane + 1], pair[:, lane + 1 : lane + 2]

    def open_chunk(chunk, carry):
        columns = columns_of(chunk)
        position = lax.broadcasted_iota(jnp.int32, (width, LANES), 0)
        for row in range(rows):
            value = orbital_ref[pl.ds(row * width, width), columns]
            for layer in range(layers_across):
                diagonal = coef_ref[row, :, 2 * layer : 2 * layer + 1]
                beside = coef_ref[row, :, 2 * layer + 1 : 2 * layer + 2]
                partner = jnp.where(
                    position % 2 == layer % 2, pltpu.roll(value, width - 1, 0), pltpu.roll(value, 1, 0)
                )
                value = diagonal * value + beside * partner
            turned[row] = value

        def pairs(step, carry):
            start = pl.multiple_of(step * BLOCK, BLOCK)
            mirrored = pl.multiple_of(width - BLOCK - step * BLOCK, BLOCK)
            place = pl.ds(start, BLOCK)
            for row in range(0, rows, 2):
                lower = turned[row, place, :]
                upper = flip(turned[row + 1, pl.ds(mirrored, BLOCK), :])
                cosine, sine = vertical(row, 0, place)
                state[chunk, row, place, :] = cosine * lower - sine * upper
                state[chunk, row + 1, place, :] = sine * lower + cosine * upper
            return carry

        lax.fori_loop(0, steps, pairs, 0)
        for copy in exchange(0, chunk):
            copy.start()
        return carry

    lax.fori_loop(0, chunks, open_chunk, 0)

    for row in range(rows):
        place = pl.ds(row * width, width)

        def turn(part, carry):
            columns = columns_of(part)
            high, low = split(jnp.transpose(trial_ref[place, columns]))
            trial_high[columns, place] = high
            trial_low[columns, place] = low
            return carry

        lax.fori_loop(0, trial_ref.shape[1] // LANES, turn, 0)

    edge_copy.wait()
    edge_coef[...] = jnp.transpose(edge_in[...])

    def crossing(stage, chunk, place):
        layer = 2 * stage + 1
        values = [state[chunk, row, place, :] for row in range(rows)]
        edge = edge_coef[place, :]
        edge_cos = edge[:, 2 * stage : 2 * stage + 1]
        edge_sin = edge[:, 2 * stage + 1 : 2 * stage + 2]
        new = list(values)
        new[0] = edge_sin * from_last[stage, chunk, place, :] + edge_cos * values[0]
        for row in range(1, rows - 1, 2):
            cosine, sine = vertical(row, layer, place)
            new[row] = cosine * values[row] - sine * values[row + 1]
            new[row + 1] = sine * values[row] + cosine * values[row + 1]
        cosine, sine = vertical(rows - 1, layer, place)
        new[rows - 1] = cosine * values[rows - 1] - sine * from_next[stage, chunk, place, :]
        return new

    own_half = pl.ds(pl.multiple_of(side * halves, 8), halves)
    other_half = pl.ds(pl.multiple_of((1 - side) * halves, 8), halves)
    own_part = pl.ds(pl.multiple_of(side * halves + chip * depth, 8), depth)

    def to_twin(chunk):
        return pltpu.make_async_remote_copy(
            src_ref=partial.at[chunk, other_half],
            dst_ref=from_twin.at[chunk],
            send_sem=twin_send.at[0, chunk],
            recv_sem=twin_recv.at[0, chunk],
            device_id={"rows": twin},
            device_id_type=pl.DeviceIdType.MESH,
        )

    def to_chip(chunk, distance):
        start = pl.multiple_of(lax.rem(chip + distance, chips) * depth, 8)
        return pltpu.make_async_remote_copy(
            src_ref=half.at[chunk, pl.ds(start, depth)],
            dst_ref=from_chips.at[chunk, distance],
            send_sem=chip_send.at[0, chunk, distance],
            recv_sem=chip_recv.at[0, chunk, distance],
            device_id={"rows": chip_at(distance)},
            device_id_type=pl.DeviceIdType.MESH,
        )

    def share(chunk, distance):
        return pltpu.make_async_remote_copy(
            src_ref=whole.at[chunk, own_part],
            dst_ref=whole.at[chunk, own_part],
            send_sem=chip_send.at[1, chunk, distance],
            recv_sem=chip_recv.at[1, chunk, distance],
            device_id={"rows": chip_at(distance)},
            device_id_type=pl.DeviceIdType.MESH,
        )

    def share_twin(chunk):
        return pltpu.make_async_remote_copy(
            src_ref=whole.at[chunk, own_half],
            dst_ref=whole.at[chunk, own_half],
            send_sem=twin_send.at[1, chunk],
            recv_sem=twin_recv.at[1, chunk],
            device_id={"rows": twin},
            device_id_type=pl.DeviceIdType.MESH,
        )

    def sum_twin(chunk):
        to_twin(chunk).wait()
        half[chunk] = partial[chunk, own_half, :] + from_twin[chunk]
        for distance in range(1, chips):
            to_chip(chunk, distance).start()

    def sum_chips(chunk):
        total = half[chunk, pl.ds(pl.multiple_of(chip * depth, 8), depth), :]
        for distance in range(1, chips):
            to_chip(chunk, distance).wait()
            total = total + from_chips[chunk, distance]
        whole[chunk, own_part, :] = total
        for distance in range(1, chips):
            share(chunk, distance).start()

    def gather_chips(chunk):
        for distance in range(1, chips):
            share(chunk, distance).wait()
        share_twin(chunk).start()

    def gather_twin(chunk):
        share_twin(chunk).wait()
        total_ref[:, columns_of(chunk)] = whole[chunk]

    for stage in range(stages):
        final = stage == stages - 1

        def advance(chunk, carry):
            for copy in exchange(stage, chunk):
                copy.wait()

            def middle(step, carry):
                place = pl.ds(pl.multiple_of(step * BLOCK, BLOCK), BLOCK)
                new = crossing(stage, chunk, place)
                for row in range(0, rows, 2):
                    cosine, sine = vertical(row, 2 * stage + 2, place)
                    state[chunk, row, place, :] = cosine * new[row] - sine * new[row + 1]
                    state[chunk, row + 1, place, :] = sine * new[row] + cosine * new[row + 1]
                return carry

            def close(step, carry):
                start = step * BLOCK
                place = pl.ds(pl.multiple_of(start, BLOCK), BLOCK)
                new = crossing(stage, chunk, place)
                for row in range(rows):
                    if row % 2:
                        at = pl.ds(pl.multiple_of((row + 1) * width - BLOCK - start, BLOCK), BLOCK)
                        evolved_ref[at, columns_of(chunk)] = flip(new[row])
                    else:
                        at = pl.ds(pl.multiple_of(row * width + start, BLOCK), BLOCK)
                        evolved_ref[at, columns_of(chunk)] = new[row]
                return carry

            lax.fori_loop(0, steps, close if final else middle, 0)
            if not final:
                for copy in exchange(stage + 1, chunk):
                    copy.start()
                return carry
            total = jnp.zeros((partial.shape[1], LANES), jnp.float32)
            for row in range(rows):
                place = pl.ds(row * width, width)
                high, low = split(evolved_ref[place, columns_of(chunk)])
                total += jnp.dot(trial_high[:, place], high, preferred_element_type=jnp.float32)
                total += jnp.dot(trial_high[:, place], low, preferred_element_type=jnp.float32)
                total += jnp.dot(trial_low[:, place], high, preferred_element_type=jnp.float32)
            partial[chunk] = total
            to_twin(chunk).start()
            return carry

        if not final:
            lax.fori_loop(0, chunks, advance, 0)
            continue

        def flow(turn, carry):
            pl.when(turn < chunks)(lambda: advance(turn, None))
            for late, work in enumerate((sum_twin, sum_chips, gather_chips, gather_twin), 1):
                pl.when((turn >= late) & (turn < chunks + late))(functools.partial(work, turn - late))
            return carry

        lax.fori_loop(0, chunks + 4, flow, 0)


def per_device(
    orbitals,
    trial_orbitals,
    angles,
    horizontal_index,
    horizontal_mask,
    vertical_index,
    vertical_mask,
):
    devices = lax.axis_size("rows")
    layers_across, rows, width = horizontal_index.shape
    layers_up = vertical_index.shape[0]
    modes, columns = orbitals.shape
    trials = trial_orbitals.shape[1]
    chunks = columns // LANES
    stages = layers_up // 2
    code = jnp.concatenate(
        [
            jnp.where(horizontal_mask == 1, horizontal_index, -1).reshape(layers_across * rows, width),
            jnp.where(vertical_mask == 1, vertical_index, -1).reshape(layers_up * rows, width),
        ],
        axis=0,
    )
    lanes = -(-2 * (layers_across + layers_up) // 8) * 8
    edges = -(-2 * stages // 8) * 8
    coef, edge = pl.pallas_call(
        functools.partial(coefficient_kernel, layers_across, layers_up, rows),
        out_shape=(
            jax.ShapeDtypeStruct((rows, width, lanes), jnp.float32),
            jax.ShapeDtypeStruct((edges, width), jnp.float32),
        ),
        name="coefficients",
    )(code, jnp.cos(angles)[None, :], jnp.sin(angles)[None, :])

    in_vmem = pl.BlockSpec(memory_space=pltpu.VMEM)
    return pl.pallas_call(
        functools.partial(step_kernel, devices, layers_across, layers_up),
        out_shape=(
            jax.ShapeDtypeStruct((modes, columns), jnp.float32),
            jax.ShapeDtypeStruct((trials, columns), jnp.float32),
        ),
        in_specs=[in_vmem] * 4,
        out_specs=(in_vmem, in_vmem),
        scratch_shapes=[
            pltpu.VMEM((chunks, rows, width, LANES), jnp.float32),
            pltpu.VMEM((stages, chunks, width, LANES), jnp.float32),
            pltpu.VMEM((stages, chunks, width, LANES), jnp.float32),
            pltpu.VMEM((edges, width), jnp.float32),
            pltpu.VMEM((width, edges), jnp.float32),
            pltpu.VMEM((rows, width, LANES), jnp.float32),
            pltpu.VMEM((trials, modes), jnp.bfloat16),
            pltpu.VMEM((trials, modes), jnp.bfloat16),
            pltpu.VMEM((chunks, trials, LANES), jnp.float32),
            pltpu.VMEM((chunks, trials // 2, LANES), jnp.float32),
            pltpu.VMEM((chunks, trials // 2, LANES), jnp.float32),
            pltpu.VMEM((chunks, devices // 2, trials // devices, LANES), jnp.float32),
            pltpu.VMEM((chunks, trials, LANES), jnp.float32),
            pltpu.SemaphoreType.DMA((stages, 2, chunks)),
            pltpu.SemaphoreType.DMA((stages, 2, chunks)),
            pltpu.SemaphoreType.DMA((2,)),
            pltpu.SemaphoreType.DMA((2, chunks)),
            pltpu.SemaphoreType.DMA((2, chunks)),
            pltpu.SemaphoreType.DMA((2, chunks, devices // 2)),
            pltpu.SemaphoreType.DMA((2, chunks, devices // 2)),
        ],
        compiler_params=pltpu.CompilerParams(
            collective_id=0, has_side_effects=True, vmem_limit_bytes=50 * 1024 * 1024
        ),
        name="trotter_step",
    )(orbitals, trial_orbitals, coef, edge)


def solution(mesh):
    in_specs = (
        P("rows", "groups"),
        P("rows", "groups"),
        P(),
        P("groups", "rows", None),
        P("groups", "rows", None),
        P("groups", "rows", None),
        P("groups", "rows", None),
    )
    out_specs = (P("rows", "groups"), P("groups", None))
    return jax.shard_map(
        per_device, mesh=mesh, in_specs=in_specs, out_specs=out_specs, check_vma=False
    )
```

```python
import functools

import jax
import jax.numpy as jnp
from jax import lax
from jax.experimental import pallas as pl
from jax.experimental.pallas import tpu as pltpu
from jax.sharding import PartitionSpec as P

LANES = 128
BLOCK = 64
IN_FLIGHT = 2


def coefficient_kernel(layers_across, layers_up, rows, across_index, across_mask, up_index, up_mask, cos_ref, sin_ref, coef_ref, edge_ref):
    code_all = jnp.concatenate(
        [
            jnp.where(mask[layer] == 1, index[layer], -1)
            for index, mask, layers in (
                (across_index, across_mask, layers_across),
                (up_index, up_mask, layers_up),
            )
            for layer in range(layers)
        ],
        axis=0,
    )
    count, width = code_all.shape
    blocks = width // LANES
    cosines, sines = [], []
    for block in range(blocks):
        code = code_all[:, block * LANES : (block + 1) * LANES]
        place = jnp.maximum(code, 0)
        table_cos = jnp.broadcast_to(cos_ref[...], code.shape)
        table_sin = jnp.broadcast_to(sin_ref[...], code.shape)
        picked_cos = jnp.take_along_axis(table_cos, place, axis=1, mode="promise_in_bounds")
        picked_sin = jnp.take_along_axis(table_sin, place, axis=1, mode="promise_in_bounds")
        cosines.append(jnp.where(code >= 0, picked_cos, 1.0))
        sines.append(jnp.where(code >= 0, picked_sin, 0.0))
    backward = LANES - 1 - lax.broadcasted_iota(jnp.int32, (count, LANES), 1)

    def reverse(parts):
        return [jnp.take_along_axis(part, backward, axis=1, mode="promise_in_bounds") for part in parts[::-1]]

    reverse_cos = jnp.concatenate(reverse(cosines), axis=1)
    reverse_sin = jnp.concatenate(reverse(sines), axis=1)
    cosine = jnp.concatenate(cosines, axis=1)
    sine = jnp.concatenate(sines, axis=1)
    position = lax.broadcasted_iota(jnp.int32, (count, width), 1)
    last_cos = pltpu.roll(cosine, 1, 1)
    last_sin = pltpu.roll(sine, 1, 1)
    diagonals, neighbours = [], []
    for layer in range(layers_across):
        first = position % 2 == layer % 2
        diagonal = jnp.where(first, cosine, last_cos)
        neighbour = jnp.where(first, -sine, last_sin)
        if layer % 2:
            inside = (position > 0) & (position < width - 1)
            diagonal = jnp.where(inside, diagonal, 1.0)
            neighbour = jnp.where(inside, neighbour, 0.0)
        diagonals.append(diagonal)
        neighbours.append(neighbour)
    lanes = coef_ref.shape[2]
    for row in range(rows):
        lines = []
        for layer in range(layers_across):
            at = layer * rows + row
            lines += [diagonals[layer][at : at + 1], neighbours[layer][at : at + 1]]
        for layer in range(layers_up):
            at = (layers_across + layer) * rows + row
            from_cos, from_sin = (reverse_cos, reverse_sin) if row % 2 else (cosine, sine)
            lines += [from_cos[at : at + 1], from_sin[at : at + 1]]
        lines.append(jnp.zeros((lanes - len(lines), width), jnp.float32))
        coef_ref[row] = jnp.transpose(jnp.concatenate(lines, axis=0))
    edges = []
    for layer in range(1, layers_up, 2):
        at = (layers_across + layer) * rows + rows - 1
        edges += [reverse_cos[at : at + 1], reverse_sin[at : at + 1]]
    spare = edge_ref.shape[0] - len(edges)
    if spare:
        edges.append(jnp.zeros((spare, width), jnp.float32))
    edge_ref[...] = jnp.concatenate(edges, axis=0)


def flip(block):
    size, columns = block.shape
    view = block.reshape(size // 8, 8, columns)
    place = lax.broadcasted_iota(jnp.int32, view.shape, 1)
    view = jnp.where(place % 2 == 0, pltpu.roll(view, 7, 1), pltpu.roll(view, 1, 1))
    view = jnp.where(place % 4 < 2, pltpu.roll(view, 6, 1), pltpu.roll(view, 2, 1))
    view = pltpu.roll(view, 4, 1)
    view = jnp.concatenate([view[k : k + 1] for k in range(size // 8)][::-1], axis=0)
    return view.reshape(size, columns)


def split(value):
    high = value.astype(jnp.bfloat16)
    low = (value - high.astype(jnp.float32)).astype(jnp.bfloat16)
    return high, low


def step_kernel(
    devices,
    layers_across,
    layers_up,
    orbital_source,
    trial_source,
    coef_ref,
    edge_ref,
    evolved_ref,
    total_ref,
    state,
    from_last,
    from_next,
    edge_in,
    edge_coef,
    turned,
    wide_across,
    wide_up,
    trial_high,
    trial_low,
    partial,
    from_twin,
    half,
    from_chips,
    own,
    from_near,
    whole,
    send_sem,
    recv_sem,
    edge_sem,
    twin_send,
    twin_recv,
    chip_send,
    chip_recv,
    near_sem,
    orbital_ref,
    trial_ref,
    load_sem,
):
    rows, width = coef_ref.shape[0], coef_ref.shape[1]
    chunks = state.shape[0]
    steps = width // BLOCK
    stages = layers_up // 2
    me = lax.axis_index("rows")
    after = lax.rem(me + 1, devices)
    before = lax.rem(me + devices - 1, devices)
    side = lax.rem(me, 2)
    twin = me + 1 - 2 * side
    far_count = devices // 4
    far = me // 4
    near = lax.rem(me // 2, 2)
    opposite = me + 2 - 4 * near
    depth = partial.shape[1] // 2 // far_count
    halves = partial.shape[1] // 2

    def chip_at(distance):
        return 4 * lax.rem(far + distance, far_count) + 2 * near + side

    def columns_of(chunk):
        return pl.ds(pl.multiple_of(chunk * LANES, LANES), LANES)

    def load(chunk):
        return pltpu.make_async_copy(
            orbital_source.at[:, columns_of(chunk)], orbital_ref.at[chunk], load_sem.at[chunk]
        )

    load_trial = pltpu.make_async_copy(trial_source, trial_ref, load_sem.at[chunks])
    for chunk in range(chunks):
        load(chunk).start()
    load_trial.start()

    barrier = pltpu.get_barrier_semaphore()
    for neighbour in (before, after, opposite):
        pl.semaphore_signal(barrier, inc=1, device_id={"rows": neighbour}, device_id_type=pl.DeviceIdType.MESH)
    for distance in range(1, far_count):
        pl.semaphore_signal(
            barrier, inc=1, device_id={"rows": chip_at(distance)}, device_id_type=pl.DeviceIdType.MESH
        )
    pl.semaphore_wait(barrier, 2 + far_count)

    edge_copy = pltpu.make_async_remote_copy(
        src_ref=edge_ref,
        dst_ref=edge_in,
        send_sem=edge_sem.at[0],
        recv_sem=edge_sem.at[1],
        device_id={"rows": after},
        device_id_type=pl.DeviceIdType.MESH,
    )
    edge_copy.start()

    def exchange(stage, chunk):
        down = pltpu.make_async_remote_copy(
            src_ref=state.at[chunk, 0],
            dst_ref=from_next.at[stage, chunk],
            send_sem=send_sem.at[stage, 0, chunk],
            recv_sem=recv_sem.at[stage, 0, chunk],
            device_id={"rows": before},
            device_id_type=pl.DeviceIdType.MESH,
        )
        up = pltpu.make_async_remote_copy(
            src_ref=state.at[chunk, rows - 1],
            dst_ref=from_last.at[stage, chunk],
            send_sem=send_sem.at[stage, 1, chunk],
            recv_sem=recv_sem.at[stage, 1, chunk],
            device_id={"rows": after},
            device_id_type=pl.DeviceIdType.MESH,
        )
        return down, up

    def begin(stage, chunk):
        for copy in exchange(stage, chunk):
            copy.start()

    def widen(line, shape=(BLOCK, LANES)):
        return jnp.broadcast_to(line, shape)

    def widen_vertical(layer, row, place):
        lane = 2 * (layers_across + layer)
        for part in range(2):
            line = coef_ref[row, place, :][:, lane + part : lane + part + 1]
            wide_up[layer, (row + 1) // 2, part, place, :] = widen(line)

    def vertical(row, layer, place):
        slot = (row + 1) // 2
        return wide_up[layer, slot, 0, place, :], wide_up[layer, slot, 1, place, :]

    def block_at(step):
        return pl.ds(pl.multiple_of(step * BLOCK, BLOCK), BLOCK)

    def prepare(step, carry):
        place = block_at(step)
        for row in range(rows):
            lines = coef_ref[row, place, :]
            for lane in range(2 * layers_across):
                wide_across[row, lane, place, :] = widen(lines[:, lane : lane + 1])
            if row % 2 == 0:
                widen_vertical(0, row, place)
        return carry

    lax.fori_loop(0, steps, prepare, 0)
    turned[:, :, :8, :] = jnp.zeros((turned.shape[0], rows, 8, LANES), jnp.float32)
    turned[:, :, width + 8 :, :] = jnp.zeros((turned.shape[0], rows, 8, LANES), jnp.float32)

    def across(layer, row, start, chunk):
        if layer == 0:
            value = orbital_ref[chunk, pl.ds(pl.multiple_of(row * width + start, BLOCK), BLOCK), :]
        elif layer % 2 == 0:
            value = turned[layer - 1, row, pl.ds(pl.multiple_of(8 + start, 8), BLOCK), :]
        else:
            value = turned[layer - 1, row, pl.ds(pl.multiple_of(start, 8), BLOCK + 16), :]
        if layer % 2 == 0:
            view = value.reshape(BLOCK // 8, 8, LANES)
            place = lax.broadcasted_iota(jnp.int32, view.shape, 1)
            partner = jnp.where(place % 2 == 0, pltpu.roll(view, 7, 1), pltpu.roll(view, 1, 1))
            partner = partner.reshape(BLOCK, LANES)
        else:
            place = lax.broadcasted_iota(jnp.int32, value.shape, 0)
            partner = jnp.where(place % 2 == 1, pltpu.roll(value, BLOCK + 15, 0), pltpu.roll(value, 1, 0))
            partner = partner[8 : 8 + BLOCK]
            value = value[8 : 8 + BLOCK]
        at = pl.ds(pl.multiple_of(start, BLOCK), BLOCK)
        return wide_across[row, 2 * layer, at, :] * value + wide_across[row, 2 * layer + 1, at, :] * partner

    def open_chunk(chunk, carry):
        load(chunk).wait()
        for layer in range(layers_across - 1):

            def inner(step, carry):
                start = step * BLOCK
                for row in range(rows):
                    at = pl.ds(pl.multiple_of(8 + start, 8), BLOCK)
                    turned[layer, row, at, :] = across(layer, row, start, chunk)
                return carry

            lax.fori_loop(0, steps, inner, 0)

        def pairs(step, carry):
            start = step * BLOCK
            mirrored = width - BLOCK - start
            place = block_at(step)
            for row in range(0, rows, 2):
                lower = across(layers_across - 1, row, start, chunk)
                upper = flip(across(layers_across - 1, row + 1, mirrored, chunk))
                cosine, sine = vertical(row, 0, place)
                state[chunk, row, place, :] = cosine * lower - sine * upper
                state[chunk, row + 1, place, :] = sine * lower + cosine * upper
            return carry

        lax.fori_loop(0, steps, pairs, 0)
        pl.when(chunk < IN_FLIGHT)(functools.partial(begin, 0, chunk))
        return carry

    lax.fori_loop(0, chunks, open_chunk, 0)

    load_trial.wait()
    for row in range(rows):
        place = pl.ds(row * width, width)

        def turn(part, carry):
            columns = columns_of(part)
            high, low = split(jnp.transpose(trial_ref[place, columns]))
            trial_high[columns, place] = high
            trial_low[columns, place] = low
            return carry

        lax.fori_loop(0, trial_ref.shape[1] // LANES, turn, 0)

    edge_copy.wait()
    edge_coef[...] = jnp.transpose(edge_in[...])

    def prepare_later(step, carry):
        place = block_at(step)
        edge = edge_coef[place, :]
        for layer in range(1, layers_up):
            for row in range(layer % 2, rows, 2):
                widen_vertical(layer, row, place)
            if layer % 2:
                for part in range(2):
                    lane = layer - 1 + part
                    wide_up[layer, 0, part, place, :] = widen(edge[:, lane : lane + 1])
        return carry

    lax.fori_loop(0, steps, prepare_later, 0)

    def crossing(stage, chunk, place):
        layer = 2 * stage + 1
        values = [state[chunk, row, place, :] for row in range(rows)]
        edge_cos, edge_sin = vertical(0, layer, place)
        new = list(values)
        new[0] = edge_sin * from_last[stage, chunk, place, :] + edge_cos * values[0]
        for row in range(1, rows - 1, 2):
            cosine, sine = vertical(row, layer, place)
            new[row] = cosine * values[row] - sine * values[row + 1]
            new[row + 1] = sine * values[row] + cosine * values[row + 1]
        cosine, sine = vertical(rows - 1, layer, place)
        new[rows - 1] = cosine * values[rows - 1] - sine * from_next[stage, chunk, place, :]
        return new

    own_half = pl.ds(pl.multiple_of(side * halves, 8), halves)
    other_half = pl.ds(pl.multiple_of((1 - side) * halves, 8), halves)
    own_part = pl.ds(pl.multiple_of(side * halves + far * depth, 8), depth)

    def to_twin(chunk):
        return pltpu.make_async_remote_copy(
            src_ref=partial.at[chunk, other_half],
            dst_ref=from_twin.at[chunk],
            send_sem=twin_send.at[0, chunk],
            recv_sem=twin_recv.at[0, chunk],
            device_id={"rows": twin},
            device_id_type=pl.DeviceIdType.MESH,
        )

    def to_chip(chunk, distance):
        start = pl.multiple_of(lax.rem(far + distance, far_count) * depth, 8)
        return pltpu.make_async_remote_copy(
            src_ref=half.at[chunk, pl.ds(start, depth)],
            dst_ref=from_chips.at[chunk, distance],
            send_sem=chip_send.at[0, chunk, distance],
            recv_sem=chip_recv.at[0, chunk, distance],
            device_id={"rows": chip_at(distance)},
            device_id_type=pl.DeviceIdType.MESH,
        )

    def cross(chunk):
        return pltpu.make_async_remote_copy(
            src_ref=own.at[chunk],
            dst_ref=from_near.at[chunk],
            send_sem=near_sem.at[0, chunk],
            recv_sem=near_sem.at[1, chunk],
            device_id={"rows": opposite},
            device_id_type=pl.DeviceIdType.MESH,
        )

    def share(chunk, distance):
        return pltpu.make_async_remote_copy(
            src_ref=whole.at[chunk, own_part],
            dst_ref=whole.at[chunk, own_part],
            send_sem=chip_send.at[1, chunk, distance],
            recv_sem=chip_recv.at[1, chunk, distance],
            device_id={"rows": chip_at(distance)},
            device_id_type=pl.DeviceIdType.MESH,
        )

    def share_twin(chunk):
        return pltpu.make_async_remote_copy(
            src_ref=whole.at[chunk, own_half],
            dst_ref=whole.at[chunk, own_half],
            send_sem=twin_send.at[1, chunk],
            recv_sem=twin_recv.at[1, chunk],
            device_id={"rows": twin},
            device_id_type=pl.DeviceIdType.MESH,
        )

    def sum_twin(chunk):
        to_twin(chunk).wait()
        half[chunk] = partial[chunk, own_half, :] + from_twin[chunk]
        for distance in range(1, far_count):
            to_chip(chunk, distance).start()

    def sum_chips(chunk):
        total = half[chunk, pl.ds(pl.multiple_of(far * depth, 8), depth), :]
        for distance in range(1, far_count):
            to_chip(chunk, distance).wait()
            total = total + from_chips[chunk, distance]
        own[chunk] = total
        cross(chunk).start()

    def sum_near(chunk):
        cross(chunk).wait()
        whole[chunk, own_part, :] = own[chunk] + from_near[chunk]
        for distance in range(1, far_count):
            share(chunk, distance).start()

    def gather_chips(chunk):
        for distance in range(1, far_count):
            share(chunk, distance).wait()
        share_twin(chunk).start()

    def gather_twin(chunk):
        share_twin(chunk).wait()
        total_ref[:, columns_of(chunk)] = whole[chunk]

    for stage in range(stages):
        final = stage == stages - 1

        def advance(chunk, carry):
            for copy in exchange(stage, chunk):
                copy.wait()
            later = chunk + IN_FLIGHT
            pl.when(later < chunks)(functools.partial(begin, stage, later))
            if not final:
                pl.when(later >= chunks)(functools.partial(begin, stage + 1, later - chunks))

            def middle(step, carry):
                place = pl.ds(pl.multiple_of(step * BLOCK, BLOCK), BLOCK)
                new = crossing(stage, chunk, place)
                for row in range(0, rows, 2):
                    cosine, sine = vertical(row, 2 * stage + 2, place)
                    state[chunk, row, place, :] = cosine * new[row] - sine * new[row + 1]
                    state[chunk, row + 1, place, :] = sine * new[row] + cosine * new[row + 1]
                return carry

            def close(step, carry):
                start = step * BLOCK
                place = pl.ds(pl.multiple_of(start, BLOCK), BLOCK)
                new = crossing(stage, chunk, place)
                for row in range(rows):
                    if row % 2:
                        at = pl.ds(pl.multiple_of((row + 1) * width - BLOCK - start, BLOCK), BLOCK)
                        evolved_ref[at, columns_of(chunk)] = flip(new[row])
                    else:
                        at = pl.ds(pl.multiple_of(row * width + start, BLOCK), BLOCK)
                        evolved_ref[at, columns_of(chunk)] = new[row]
                return carry

            lax.fori_loop(0, steps, close if final else middle, 0)
            if not final:
                return carry
            total = jnp.zeros((partial.shape[1], LANES), jnp.float32)
            for row in range(rows):
                place = pl.ds(row * width, width)
                high, low = split(evolved_ref[place, columns_of(chunk)])
                both = jnp.concatenate([high, low], axis=1)
                both = jnp.dot(trial_high[:, place], both, preferred_element_type=jnp.float32)
                total += both[:, :LANES] + both[:, LANES:]
                total += jnp.dot(trial_low[:, place], high, preferred_element_type=jnp.float32)
            partial[chunk] = total
            to_twin(chunk).start()
            return carry

        if not final:
            lax.fori_loop(0, chunks, advance, 0)
            continue

        def flow(turn, carry):
            pl.when(turn < chunks)(lambda: advance(turn, None))
            for late, work in enumerate((sum_twin, sum_chips, sum_near, gather_chips, gather_twin), 1):
                pl.when((turn >= late) & (turn < chunks + late))(functools.partial(work, turn - late))
            return carry

        lax.fori_loop(0, chunks + 5, flow, 0)


def per_device(
    orbitals,
    trial_orbitals,
    angles,
    horizontal_index,
    horizontal_mask,
    vertical_index,
    vertical_mask,
):
    devices = lax.axis_size("rows")
    layers_across, rows, width = horizontal_index.shape
    layers_up = vertical_index.shape[0]
    modes, columns = orbitals.shape
    trials = trial_orbitals.shape[1]
    chunks = columns // LANES
    far_count = devices // 4
    stages = layers_up // 2
    lanes = -(-2 * (layers_across + layers_up) // 8) * 8
    edges = -(-2 * stages // 8) * 8
    coef, edge = pl.pallas_call(
        functools.partial(coefficient_kernel, layers_across, layers_up, rows),
        out_shape=(
            jax.ShapeDtypeStruct((rows, width, lanes), jnp.float32),
            jax.ShapeDtypeStruct((edges, width), jnp.float32),
        ),
        name="coefficients",
    )(
        horizontal_index,
        horizontal_mask,
        vertical_index,
        vertical_mask,
        jnp.cos(angles)[None, :],
        jnp.sin(angles)[None, :],
    )

    in_vmem = pl.BlockSpec(memory_space=pltpu.VMEM)
    in_hbm = pl.BlockSpec(memory_space=pl.ANY)
    return pl.pallas_call(
        functools.partial(step_kernel, devices, layers_across, layers_up),
        out_shape=(
            jax.ShapeDtypeStruct((modes, columns), jnp.float32),
            jax.ShapeDtypeStruct((trials, columns), jnp.float32),
        ),
        in_specs=[in_hbm, in_hbm, in_vmem, in_vmem],
        out_specs=(in_vmem, in_vmem),
        scratch_shapes=[
            pltpu.VMEM((chunks, rows, width, LANES), jnp.float32),
            pltpu.VMEM((stages, chunks, width, LANES), jnp.float32),
            pltpu.VMEM((stages, chunks, width, LANES), jnp.float32),
            pltpu.VMEM((edges, width), jnp.float32),
            pltpu.VMEM((width, edges), jnp.float32),
            pltpu.VMEM((max(layers_across - 1, 1), rows, width + 16, LANES), jnp.float32),
            pltpu.VMEM((rows, 2 * layers_across, width, LANES), jnp.float32),
            pltpu.VMEM((layers_up, rows // 2 + 1, 2, width, LANES), jnp.float32),
            pltpu.VMEM((trials, modes), jnp.bfloat16),
            pltpu.VMEM((trials, modes), jnp.bfloat16),
            pltpu.VMEM((chunks, trials, LANES), jnp.float32),
            pltpu.VMEM((chunks, trials // 2, LANES), jnp.float32),
            pltpu.VMEM((chunks, trials // 2, LANES), jnp.float32),
            pltpu.VMEM((chunks, far_count, trials // 2 // far_count, LANES), jnp.float32),
            pltpu.VMEM((chunks, trials // 2 // far_count, LANES), jnp.float32),
            pltpu.VMEM((chunks, trials // 2 // far_count, LANES), jnp.float32),
            pltpu.VMEM((chunks, trials, LANES), jnp.float32),
            pltpu.SemaphoreType.DMA((stages, 2, chunks)),
            pltpu.SemaphoreType.DMA((stages, 2, chunks)),
            pltpu.SemaphoreType.DMA((2,)),
            pltpu.SemaphoreType.DMA((2, chunks)),
            pltpu.SemaphoreType.DMA((2, chunks)),
            pltpu.SemaphoreType.DMA((2, chunks, far_count)),
            pltpu.SemaphoreType.DMA((2, chunks, far_count)),
            pltpu.SemaphoreType.DMA((2, chunks)),
            pltpu.VMEM((chunks, modes, LANES), jnp.float32),
            pltpu.VMEM((modes, trials), jnp.float32),
            pltpu.SemaphoreType.DMA((chunks + 1,)),
        ],
        compiler_params=pltpu.CompilerParams(
            collective_id=0, has_side_effects=True, vmem_limit_bytes=56 * 1024 * 1024
        ),
        name="trotter_step",
    )(orbitals, trial_orbitals, coef, edge)


def solution(mesh):
    in_specs = (
        P("rows", "groups"),
        P("rows", "groups"),
        P(),
        P("groups", "rows", None),
        P("groups", "rows", None),
        P("groups", "rows", None),
        P("groups", "rows", None),
    )
    out_specs = (P("rows", "groups"), P("groups", None))
    return jax.shard_map(
        per_device, mesh=mesh, in_specs=in_specs, out_specs=out_specs, check_vma=False
    )
```

```python
import functools

import jax
import jax.numpy as jnp
from jax import lax
from jax.experimental import pallas as pl
from jax.experimental.pallas import tpu as pltpu
from jax.sharding import PartitionSpec as P

LANES = 128
BLOCK = 128
IN_FLIGHT = 3


def coefficient_kernel(layers_across, layers_up, rows, across_index, across_mask, up_index, up_mask, cos_ref, sin_ref, coef_ref, edge_ref):
    code_all = jnp.concatenate(
        [
            jnp.where(mask[layer] == 1, index[layer], -1)
            for index, mask, layers in (
                (across_index, across_mask, layers_across),
                (up_index, up_mask, layers_up),
            )
            for layer in range(layers)
        ],
        axis=0,
    )
    count, width = code_all.shape
    blocks = width // LANES
    cosines, sines = [], []
    for block in range(blocks):
        code = code_all[:, block * LANES : (block + 1) * LANES]
        place = jnp.maximum(code, 0)
        table_cos = jnp.broadcast_to(cos_ref[...], code.shape)
        table_sin = jnp.broadcast_to(sin_ref[...], code.shape)
        picked_cos = jnp.take_along_axis(table_cos, place, axis=1, mode="promise_in_bounds")
        picked_sin = jnp.take_along_axis(table_sin, place, axis=1, mode="promise_in_bounds")
        cosines.append(jnp.where(code >= 0, picked_cos, 1.0))
        sines.append(jnp.where(code >= 0, picked_sin, 0.0))
    backward = LANES - 1 - lax.broadcasted_iota(jnp.int32, (count, LANES), 1)

    def reverse(parts):
        return [jnp.take_along_axis(part, backward, axis=1, mode="promise_in_bounds") for part in parts[::-1]]

    reverse_cos = jnp.concatenate(reverse(cosines), axis=1)
    reverse_sin = jnp.concatenate(reverse(sines), axis=1)
    cosine = jnp.concatenate(cosines, axis=1)
    sine = jnp.concatenate(sines, axis=1)
    position = lax.broadcasted_iota(jnp.int32, (count, width), 1)
    last_cos = pltpu.roll(cosine, 1, 1)
    last_sin = pltpu.roll(sine, 1, 1)
    diagonals, neighbours = [], []
    for layer in range(layers_across):
        first = position % 2 == layer % 2
        diagonal = jnp.where(first, cosine, last_cos)
        neighbour = jnp.where(first, -sine, last_sin)
        if layer % 2:
            inside = (position > 0) & (position < width - 1)
            diagonal = jnp.where(inside, diagonal, 1.0)
            neighbour = jnp.where(inside, neighbour, 0.0)
        diagonals.append(diagonal)
        neighbours.append(neighbour)
    lanes = coef_ref.shape[2]
    for row in range(rows):
        lines = []
        for layer in range(layers_across):
            at = layer * rows + row
            lines += [diagonals[layer][at : at + 1], neighbours[layer][at : at + 1]]
        for layer in range(layers_up):
            at = (layers_across + layer) * rows + row
            from_cos, from_sin = (reverse_cos, reverse_sin) if row % 2 else (cosine, sine)
            lines += [from_cos[at : at + 1], from_sin[at : at + 1]]
        lines.append(jnp.zeros((lanes - len(lines), width), jnp.float32))
        coef_ref[row] = jnp.transpose(jnp.concatenate(lines, axis=0))
    edges = []
    for layer in range(1, layers_up, 2):
        at = (layers_across + layer) * rows + rows - 1
        edges += [reverse_cos[at : at + 1], reverse_sin[at : at + 1]]
    spare = edge_ref.shape[0] - len(edges)
    if spare:
        edges.append(jnp.zeros((spare, width), jnp.float32))
    edge_ref[...] = jnp.concatenate(edges, axis=0)


def flip(block):
    size, columns = block.shape
    view = block.reshape(size // 8, 8, columns)
    place = lax.broadcasted_iota(jnp.int32, view.shape, 1)
    view = jnp.where(place % 2 == 0, pltpu.roll(view, 7, 1), pltpu.roll(view, 1, 1))
    view = jnp.where(place % 4 < 2, pltpu.roll(view, 6, 1), pltpu.roll(view, 2, 1))
    view = pltpu.roll(view, 4, 1)
    view = jnp.concatenate([view[k : k + 1] for k in range(size // 8)][::-1], axis=0)
    return view.reshape(size, columns)


def split(value):
    high = value.astype(jnp.bfloat16)
    low = (value - high.astype(jnp.float32)).astype(jnp.bfloat16)
    return high, low


def step_kernel(
    devices,
    layers_across,
    layers_up,
    orbital_source,
    trial_source,
    coef_ref,
    edge_ref,
    evolved_target,
    total_ref,
    state,
    from_last,
    from_next,
    edge_in,
    edge_coef,
    turned,
    wide_across,
    wide_up,
    trial_high,
    trial_low,
    partial,
    from_twin,
    half,
    from_chips,
    own,
    from_near,
    whole,
    send_sem,
    recv_sem,
    edge_sem,
    twin_send,
    twin_recv,
    chip_send,
    chip_recv,
    near_sem,
    orbital_ref,
    trial_ref,
    load_sem,
    evolved_ref,
    store_sem,
):
    rows, width = coef_ref.shape[0], coef_ref.shape[1]
    chunks = state.shape[0]
    steps = width // BLOCK
    stages = layers_up // 2
    me = lax.axis_index("rows")
    after = lax.rem(me + 1, devices)
    before = lax.rem(me + devices - 1, devices)
    side = lax.rem(me, 2)
    twin = me + 1 - 2 * side
    far_count = devices // 4
    far = me // 4
    near = lax.rem(me // 2, 2)
    opposite = me + 2 - 4 * near
    depth = partial.shape[1] // 2 // far_count
    halves = partial.shape[1] // 2

    def chip_at(distance):
        return 4 * lax.rem(far + distance, far_count) + 2 * near + side

    def columns_of(chunk):
        return pl.ds(pl.multiple_of(chunk * LANES, LANES), LANES)

    def load(chunk):
        return pltpu.make_async_copy(
            orbital_source.at[:, columns_of(chunk)], orbital_ref.at[chunk], load_sem.at[chunk]
        )

    def store(chunk):
        return pltpu.make_async_copy(
            evolved_ref.at[chunk], evolved_target.at[:, columns_of(chunk)], store_sem.at[chunk]
        )

    load_trial = pltpu.make_async_copy(trial_source, trial_ref, load_sem.at[chunks])
    for chunk in range(chunks):
        load(chunk).start()
    load_trial.start()

    barrier = pltpu.get_barrier_semaphore()
    for neighbour in (before, after, opposite):
        pl.semaphore_signal(barrier, inc=1, device_id={"rows": neighbour}, device_id_type=pl.DeviceIdType.MESH)
    for distance in range(1, far_count):
        pl.semaphore_signal(
            barrier, inc=1, device_id={"rows": chip_at(distance)}, device_id_type=pl.DeviceIdType.MESH
        )
    pl.semaphore_wait(barrier, 2 + far_count)

    edge_copy = pltpu.make_async_remote_copy(
        src_ref=edge_ref,
        dst_ref=edge_in,
        send_sem=edge_sem.at[0],
        recv_sem=edge_sem.at[1],
        device_id={"rows": after},
        device_id_type=pl.DeviceIdType.MESH,
    )
    edge_copy.start()

    def exchange(stage, chunk):
        down = pltpu.make_async_remote_copy(
            src_ref=state.at[chunk, 0],
            dst_ref=from_next.at[stage, chunk],
            send_sem=send_sem.at[stage, 0, chunk],
            recv_sem=recv_sem.at[stage, 0, chunk],
            device_id={"rows": before},
            device_id_type=pl.DeviceIdType.MESH,
        )
        up = pltpu.make_async_remote_copy(
            src_ref=state.at[chunk, rows - 1],
            dst_ref=from_last.at[stage, chunk],
            send_sem=send_sem.at[stage, 1, chunk],
            recv_sem=recv_sem.at[stage, 1, chunk],
            device_id={"rows": after},
            device_id_type=pl.DeviceIdType.MESH,
        )
        return down, up

    def begin(stage, chunk):
        for copy in exchange(stage, chunk):
            copy.start()

    def widen(line, shape=(BLOCK, LANES)):
        return jnp.broadcast_to(line, shape)

    def widen_vertical(layer, row, place):
        lane = 2 * (layers_across + layer)
        for part in range(2):
            line = coef_ref[row, place, :][:, lane + part : lane + part + 1]
            wide_up[layer, (row + 1) // 2, part, place, :] = widen(line)

    def vertical(row, layer, place):
        slot = (row + 1) // 2
        return wide_up[layer, slot, 0, place, :], wide_up[layer, slot, 1, place, :]

    def block_at(step):
        return pl.ds(pl.multiple_of(step * BLOCK, BLOCK), BLOCK)

    def prepare(step, carry):
        place = block_at(step)
        for row in range(rows):
            lines = coef_ref[row, place, :]
            for lane in range(2 * layers_across):
                wide_across[row, lane, place, :] = widen(lines[:, lane : lane + 1])
            if row % 2 == 0:
                widen_vertical(0, row, place)
        return carry

    lax.fori_loop(0, steps, prepare, 0)
    turned[:, :, :8, :] = jnp.zeros((turned.shape[0], rows, 8, LANES), jnp.float32)
    turned[:, :, width + 8 :, :] = jnp.zeros((turned.shape[0], rows, 8, LANES), jnp.float32)

    def across(layer, row, start, chunk):
        if layer == 0:
            value = orbital_ref[chunk, pl.ds(pl.multiple_of(row * width + start, BLOCK), BLOCK), :]
        elif layer % 2 == 0:
            value = turned[layer - 1, row, pl.ds(pl.multiple_of(8 + start, 8), BLOCK), :]
        else:
            value = turned[layer - 1, row, pl.ds(pl.multiple_of(start, 8), BLOCK + 16), :]
        if layer % 2 == 0:
            view = value.reshape(BLOCK // 8, 8, LANES)
            place = lax.broadcasted_iota(jnp.int32, view.shape, 1)
            partner = jnp.where(place % 2 == 0, pltpu.roll(view, 7, 1), pltpu.roll(view, 1, 1))
            partner = partner.reshape(BLOCK, LANES)
        else:
            place = lax.broadcasted_iota(jnp.int32, value.shape, 0)
            partner = jnp.where(place % 2 == 1, pltpu.roll(value, BLOCK + 15, 0), pltpu.roll(value, 1, 0))
            partner = partner[8 : 8 + BLOCK]
            value = value[8 : 8 + BLOCK]
        at = pl.ds(pl.multiple_of(start, BLOCK), BLOCK)
        return wide_across[row, 2 * layer, at, :] * value + wide_across[row, 2 * layer + 1, at, :] * partner

    def open_chunk(chunk, carry):
        load(chunk).wait()
        for layer in range(layers_across - 1):

            def inner(step, carry):
                start = step * BLOCK
                for row in range(rows):
                    at = pl.ds(pl.multiple_of(8 + start, 8), BLOCK)
                    turned[layer, row, at, :] = across(layer, row, start, chunk)
                return carry

            lax.fori_loop(0, steps, inner, 0)

        def pairs(step, carry):
            start = step * BLOCK
            mirrored = width - BLOCK - start
            place = block_at(step)
            for row in range(0, rows, 2):
                lower = across(layers_across - 1, row, start, chunk)
                upper = flip(across(layers_across - 1, row + 1, mirrored, chunk))
                cosine, sine = vertical(row, 0, place)
                state[chunk, row, place, :] = cosine * lower - sine * upper
                state[chunk, row + 1, place, :] = sine * lower + cosine * upper
            return carry

        lax.fori_loop(0, steps, pairs, 0)
        pl.when(chunk < IN_FLIGHT)(functools.partial(begin, 0, chunk))
        return carry

    lax.fori_loop(0, chunks, open_chunk, 0)

    load_trial.wait()
    for row in range(rows):
        place = pl.ds(row * width, width)

        def turn(part, carry):
            columns = columns_of(part)
            high, low = split(jnp.transpose(trial_ref[place, columns]))
            trial_high[columns, place] = high
            trial_low[columns, place] = low
            return carry

        lax.fori_loop(0, trial_ref.shape[1] // LANES, turn, 0)

    edge_copy.wait()
    edge_coef[...] = jnp.transpose(edge_in[...])

    def prepare_later(step, carry):
        place = block_at(step)
        edge = edge_coef[place, :]
        for layer in range(1, layers_up):
            for row in range(layer % 2, rows, 2):
                widen_vertical(layer, row, place)
            if layer % 2:
                for part in range(2):
                    lane = layer - 1 + part
                    wide_up[layer, 0, part, place, :] = widen(edge[:, lane : lane + 1])
        return carry

    lax.fori_loop(0, steps, prepare_later, 0)

    def crossing(stage, chunk, place):
        layer = 2 * stage + 1
        values = [state[chunk, row, place, :] for row in range(rows)]
        edge_cos, edge_sin = vertical(0, layer, place)
        new = list(values)
        new[0] = edge_sin * from_last[stage, chunk, place, :] + edge_cos * values[0]
        for row in range(1, rows - 1, 2):
            cosine, sine = vertical(row, layer, place)
            new[row] = cosine * values[row] - sine * values[row + 1]
            new[row + 1] = sine * values[row] + cosine * values[row + 1]
        cosine, sine = vertical(rows - 1, layer, place)
        new[rows - 1] = cosine * values[rows - 1] - sine * from_next[stage, chunk, place, :]
        return new

    own_half = pl.ds(pl.multiple_of(side * halves, 8), halves)
    other_half = pl.ds(pl.multiple_of((1 - side) * halves, 8), halves)
    own_part = pl.ds(pl.multiple_of(side * halves + far * depth, 8), depth)

    def to_twin(chunk):
        return pltpu.make_async_remote_copy(
            src_ref=partial.at[chunk, other_half],
            dst_ref=from_twin.at[chunk],
            send_sem=twin_send.at[0, chunk],
            recv_sem=twin_recv.at[0, chunk],
            device_id={"rows": twin},
            device_id_type=pl.DeviceIdType.MESH,
        )

    def to_chip(chunk, distance):
        start = pl.multiple_of(lax.rem(far + distance, far_count) * depth, 8)
        return pltpu.make_async_remote_copy(
            src_ref=half.at[chunk, pl.ds(start, depth)],
            dst_ref=from_chips.at[chunk, distance],
            send_sem=chip_send.at[0, chunk, distance],
            recv_sem=chip_recv.at[0, chunk, distance],
            device_id={"rows": chip_at(distance)},
            device_id_type=pl.DeviceIdType.MESH,
        )

    def cross(chunk):
        return pltpu.make_async_remote_copy(
            src_ref=own.at[chunk],
            dst_ref=from_near.at[chunk],
            send_sem=near_sem.at[0, chunk],
            recv_sem=near_sem.at[1, chunk],
            device_id={"rows": opposite},
            device_id_type=pl.DeviceIdType.MESH,
        )

    def share(chunk, distance):
        return pltpu.make_async_remote_copy(
            src_ref=whole.at[chunk, own_part],
            dst_ref=whole.at[chunk, own_part],
            send_sem=chip_send.at[1, chunk, distance],
            recv_sem=chip_recv.at[1, chunk, distance],
            device_id={"rows": chip_at(distance)},
            device_id_type=pl.DeviceIdType.MESH,
        )

    def share_twin(chunk):
        return pltpu.make_async_remote_copy(
            src_ref=whole.at[chunk, own_half],
            dst_ref=whole.at[chunk, own_half],
            send_sem=twin_send.at[1, chunk],
            recv_sem=twin_recv.at[1, chunk],
            device_id={"rows": twin},
            device_id_type=pl.DeviceIdType.MESH,
        )

    def sum_twin(chunk):
        to_twin(chunk).wait()
        half[chunk] = partial[chunk, own_half, :] + from_twin[chunk]
        for distance in range(1, far_count):
            to_chip(chunk, distance).start()

    def sum_chips(chunk):
        total = half[chunk, pl.ds(pl.multiple_of(far * depth, 8), depth), :]
        for distance in range(1, far_count):
            to_chip(chunk, distance).wait()
            total = total + from_chips[chunk, distance]
        own[chunk] = total
        cross(chunk).start()

    def sum_near(chunk):
        cross(chunk).wait()
        whole[chunk, own_part, :] = own[chunk] + from_near[chunk]
        for distance in range(1, far_count):
            share(chunk, distance).start()

    def gather_chips(chunk):
        for distance in range(1, far_count):
            share(chunk, distance).wait()
        share_twin(chunk).start()

    def gather_twin(chunk):
        share_twin(chunk).wait()
        total_ref[:, columns_of(chunk)] = whole[chunk]

    for stage in range(stages):
        final = stage == stages - 1

        def advance(chunk, carry):
            for copy in exchange(stage, chunk):
                copy.wait()
            later = chunk + IN_FLIGHT
            pl.when(later < chunks)(functools.partial(begin, stage, later))
            if not final:
                pl.when(later >= chunks)(functools.partial(begin, stage + 1, later - chunks))

            def middle(step, carry):
                place = pl.ds(pl.multiple_of(step * BLOCK, BLOCK), BLOCK)
                new = crossing(stage, chunk, place)
                for row in range(0, rows, 2):
                    cosine, sine = vertical(row, 2 * stage + 2, place)
                    state[chunk, row, place, :] = cosine * new[row] - sine * new[row + 1]
                    state[chunk, row + 1, place, :] = sine * new[row] + cosine * new[row + 1]
                return carry

            def close(step, carry):
                start = step * BLOCK
                place = pl.ds(pl.multiple_of(start, BLOCK), BLOCK)
                new = crossing(stage, chunk, place)
                for row in range(rows):
                    if row % 2:
                        at = pl.ds(pl.multiple_of((row + 1) * width - BLOCK - start, BLOCK), BLOCK)
                        evolved_ref[chunk, at, :] = flip(new[row])
                    else:
                        at = pl.ds(pl.multiple_of(row * width + start, BLOCK), BLOCK)
                        evolved_ref[chunk, at, :] = new[row]
                return carry

            lax.fori_loop(0, steps, close if final else middle, 0)
            if not final:
                return carry
            store(chunk).start()
            total = jnp.zeros((partial.shape[1], LANES), jnp.float32)
            for row in range(rows):
                place = pl.ds(row * width, width)
                high, low = split(evolved_ref[chunk, place, :])
                both = jnp.concatenate([high, low], axis=1)
                both = jnp.dot(trial_high[:, place], both, preferred_element_type=jnp.float32)
                total += both[:, :LANES] + both[:, LANES:]
                total += jnp.dot(trial_low[:, place], high, preferred_element_type=jnp.float32)
            partial[chunk] = total
            to_twin(chunk).start()
            return carry

        if not final:
            lax.fori_loop(0, chunks, advance, 0)
            continue

        def flow(turn, carry):
            pl.when(turn < chunks)(lambda: advance(turn, None))
            for late, work in enumerate((sum_twin, sum_chips, sum_near, gather_chips, gather_twin), 1):
                pl.when((turn >= late) & (turn < chunks + late))(functools.partial(work, turn - late))
            return carry

        lax.fori_loop(0, chunks + 5, flow, 0)
        for chunk in range(chunks):
            store(chunk).wait()


def per_device(
    orbitals,
    trial_orbitals,
    angles,
    horizontal_index,
    horizontal_mask,
    vertical_index,
    vertical_mask,
):
    devices = lax.axis_size("rows")
    layers_across, rows, width = horizontal_index.shape
    layers_up = vertical_index.shape[0]
    modes, columns = orbitals.shape
    trials = trial_orbitals.shape[1]
    chunks = columns // LANES
    far_count = devices // 4
    stages = layers_up // 2
    lanes = -(-2 * (layers_across + layers_up) // 8) * 8
    edges = -(-2 * stages // 8) * 8
    coef, edge = pl.pallas_call(
        functools.partial(coefficient_kernel, layers_across, layers_up, rows),
        out_shape=(
            jax.ShapeDtypeStruct((rows, width, lanes), jnp.float32),
            jax.ShapeDtypeStruct((edges, width), jnp.float32),
        ),
        name="coefficients",
    )(
        horizontal_index,
        horizontal_mask,
        vertical_index,
        vertical_mask,
        jnp.cos(angles)[None, :],
        jnp.sin(angles)[None, :],
    )

    in_vmem = pl.BlockSpec(memory_space=pltpu.VMEM)
    in_hbm = pl.BlockSpec(memory_space=pl.ANY)
    return pl.pallas_call(
        functools.partial(step_kernel, devices, layers_across, layers_up),
        out_shape=(
            jax.ShapeDtypeStruct((modes, columns), jnp.float32),
            jax.ShapeDtypeStruct((trials, columns), jnp.float32),
        ),
        in_specs=[in_hbm, in_hbm, in_vmem, in_vmem],
        out_specs=(in_hbm, in_vmem),
        scratch_shapes=[
            pltpu.VMEM((chunks, rows, width, LANES), jnp.float32),
            pltpu.VMEM((stages, chunks, width, LANES), jnp.float32),
            pltpu.VMEM((stages, chunks, width, LANES), jnp.float32),
            pltpu.VMEM((edges, width), jnp.float32),
            pltpu.VMEM((width, edges), jnp.float32),
            pltpu.VMEM((max(layers_across - 1, 1), rows, width + 16, LANES), jnp.float32),
            pltpu.VMEM((rows, 2 * layers_across, width, LANES), jnp.float32),
            pltpu.VMEM((layers_up, rows // 2 + 1, 2, width, LANES), jnp.float32),
            pltpu.VMEM((trials, modes), jnp.bfloat16),
            pltpu.VMEM((trials, modes), jnp.bfloat16),
            pltpu.VMEM((chunks, trials, LANES), jnp.float32),
            pltpu.VMEM((chunks, trials // 2, LANES), jnp.float32),
            pltpu.VMEM((chunks, trials // 2, LANES), jnp.float32),
            pltpu.VMEM((chunks, far_count, trials // 2 // far_count, LANES), jnp.float32),
            pltpu.VMEM((chunks, trials // 2 // far_count, LANES), jnp.float32),
            pltpu.VMEM((chunks, trials // 2 // far_count, LANES), jnp.float32),
            pltpu.VMEM((chunks, trials, LANES), jnp.float32),
            pltpu.SemaphoreType.DMA((stages, 2, chunks)),
            pltpu.SemaphoreType.DMA((stages, 2, chunks)),
            pltpu.SemaphoreType.DMA((2,)),
            pltpu.SemaphoreType.DMA((2, chunks)),
            pltpu.SemaphoreType.DMA((2, chunks)),
            pltpu.SemaphoreType.DMA((2, chunks, far_count)),
            pltpu.SemaphoreType.DMA((2, chunks, far_count)),
            pltpu.SemaphoreType.DMA((2, chunks)),
            pltpu.VMEM((chunks, modes, LANES), jnp.float32),
            pltpu.VMEM((modes, trials), jnp.float32),
            pltpu.SemaphoreType.DMA((chunks + 1,)),
            pltpu.VMEM((chunks, modes, LANES), jnp.float32),
            pltpu.SemaphoreType.DMA((chunks,)),
        ],
        compiler_params=pltpu.CompilerParams(
            collective_id=0, has_side_effects=True, vmem_limit_bytes=56 * 1024 * 1024
        ),
        name="trotter_step",
    )(orbitals, trial_orbitals, coef, edge)


def solution(mesh):
    in_specs = (
        P("rows", "groups"),
        P("rows", "groups"),
        P(),
        P("groups", "rows", None),
        P("groups", "rows", None),
        P("groups", "rows", None),
        P("groups", "rows", None),
    )
    out_specs = (P("rows", "groups"), P("groups", None))
    return jax.shard_map(
        per_device, mesh=mesh, in_specs=in_specs, out_specs=out_specs, check_vma=False
    )
```
